32 devices in a mesh: freq: 2 (over x), space: 16 (over z, y, core).
Axes of the slice: x: 2, y: 2, z: 4, core: 2. Of those that a mesh axis runs over, the one named last changes fastest.
Arguments:
- rhs: float32 [2, 5, 256, 1024], P(None, None, ('freq', 'space')), parts along dimension 2, may hold values from -12 to 12
- inv_diag: float32 [2, 5, 5, 256, 1024], P(None, None, None, ('freq', 'space')), parts along dimension 3
- face_coef: float32 [4, 256, 1024], P(None, ('freq', 'space')), parts along dimension 1, may hold values from 0.6 to 1.8
- flux_jac: float32 [2, 5, 5], replicated, may hold values from -1.8 to 1.8
- press_weights: float32 [5], replicated, may hold values from -4 to 4
- surface_cells: int32 [8192], P('space'), may hold values from 0 to 8191, as said below
- interface_slot: int32 [8192], P('space'), may hold values from 0 to 8191, as said below
- mode_shapes: float32 [8192, 192], P('space'), may hold values from -0.09375 to 0.09375
Outputs:
- state: float32 [2, 5, 256, 1024], P(None, None, ('freq', 'space')), parts along dimension 2
- forces: float32 [2, 384], P(None, ('freq', 'space')), parts along dimension 1
The draws below stay inside these ranges and needn't reach their ends.
There are 2 independent parts, one for each index of `freq`. The reference program is written for one: setup_inputs(seed, part) draws one part's arguments, and reference() takes and returns one part's arrays. A program takes and returns all parts, laid end to end along the dimension named above; an argument that names none is the same for every part. Nothing has to cross between parts.
Inputs may be any that keep to these rules, and one draw needn't show every extreme that they name: `surface_cells`: the 512 entries held by one device are distinct cell indices of that device; on some device they include both its first and its last cell. `interface_slot`: A permutation of all 8192 interface indices; the owner of index i is device i // 512 of space, and each device holds exactly the same number of rows of every owner.
All inputs are finite; a program needn't handle non-finite values.
Results may differ from the reference program's by a relative error of at most 0.0003.
Values sent between devices are 32-bit elements; how exact they have to be, the bound alone decides.
A program may use at most 64 MiB of HBM per device.

```python
import jax
import jax.numpy as jnp
from jax import lax

COMP = 5
NP = 8
NQ = 1024
SD = 512
MODES = 192
ITERS = 8
NPT = 128
SURF = 8192
N_SPACE = 16


def draw_inv_diag(key, part):
    key_scale = jax.random.fold_in(key, 11)
    key_noise = jax.random.fold_in(key, 12)
    key_phase = jax.random.fold_in(key, 13)
    scales = jnp.exp(jax.random.uniform(key_scale, (NPT, NQ), jnp.float32, jnp.log(0.25), jnp.log(0.5)))
    noise = 0.25 * jax.random.normal(key_noise, (2, 5, 5, NPT, NQ), jnp.float32)
    identity = jnp.eye(5, dtype=jnp.float32)[:, :, None, None]
    phases = jax.random.uniform(key_phase, (NPT, NQ), jnp.float32, -0.6, 0.6)
    diagonal = jnp.stack([identity * jnp.ones((NPT, NQ), jnp.float32), identity * phases])
    return (scales * (diagonal + noise)).astype(jnp.float32)


def draw_surface_cells(key, part):
    total = NP * NQ
    device_keys = jax.random.split(jax.random.fold_in(key, 21), N_SPACE)
    drawn = jax.vmap(lambda single: jax.random.permutation(single, total)[:SD])(device_keys)
    chosen = jax.random.randint(jax.random.fold_in(key, 22), (), 0, N_SPACE)
    inner = jax.random.permutation(jax.random.fold_in(key, 23), total - 2)[:SD - 2].astype(jnp.int32) + 1
    ends = jnp.array([0, total - 1], dtype=jnp.int32)
    special = jax.random.permutation(jax.random.fold_in(key, 24), jnp.concatenate([ends, inner]))
    rows = jnp.arange(N_SPACE, dtype=jnp.int32)[:, None]
    picks = jnp.where(rows == chosen, special[None].astype(jnp.int32), drawn.astype(jnp.int32))
    return picks.reshape(-1).astype(jnp.int32)


def draw_interface_slot(key, part):
    share = SD // N_SPACE
    owner_keys = jax.random.split(jax.random.fold_in(key, 31), N_SPACE)
    owned = jax.vmap(lambda single: jax.random.permutation(single, SD))(owner_keys)
    owned = owned.astype(jnp.int32) + (jnp.arange(N_SPACE, dtype=jnp.int32) * SD)[:, None]
    blocks = owned.reshape(N_SPACE, N_SPACE, share).transpose(1, 0, 2).reshape(N_SPACE, SD)
    source_keys = jax.random.split(jax.random.fold_in(key, 32), N_SPACE)
    shuffled = jax.vmap(lambda single, values: jax.random.permutation(single, values))(source_keys, blocks)
    return shuffled.reshape(-1).astype(jnp.int32)


def raised(result, key, source, target, parts, factor):
    owner, partner = [(jnp.arange(result.shape[dim]) // (result.shape[dim] // parts)).reshape([-1 if axis == dim else 1 for axis in range(result.ndim)]) for dim in (source, target)]
    chosen = jax.random.permutation(key, parts)[partner]
    strong = (owner == chosen) | (owner == (partner + parts // 2) % parts)
    return jnp.where(strong, factor * result, result)


def level_of(stream_key, shape, cuts, least, high):
    def one(position, blocks):
        heights = jax.random.uniform(jax.random.fold_in(jax.random.fold_in(stream_key, 6), position), (blocks,), jnp.float32, least / len(cuts), high / len(cuts))
        return jnp.repeat(jnp.exp(heights), shape[position] // blocks).reshape((-1,) + (1,) * (len(shape) - position - 1))

    level = one(*cuts[0])
    for cut in cuts[1:]:
        level = level * one(*cut)
    return level


def gaussian(key, extent, spread, limit, pieces=(), kind=jnp.bfloat16):
    level = level_of(key, extent, pieces, -0.22, 0.18) if pieces else 1.0
    drawn = jax.random.normal(key, extent, jnp.float32) * spread * level
    return jnp.minimum(jnp.maximum(drawn, -limit), limit).astype(kind)


def bell_draw_with(key, shape, width, limit, cuts, heavy, held_as=jnp.bfloat16):
    result = width * jax.random.normal(key, shape, jnp.float32)
    if cuts:
        result = result * level_of(key, shape, cuts, -0.22, 0.18)
    return jnp.clip(raised(result, jax.random.fold_in(key, 3), *heavy), -limit, limit).astype(held_as)


def setup_inputs(seed: int = 0, part: int = 0) -> dict:
    key_list = jax.random.split(jax.random.key(seed), 9)
    part_keys = jax.random.split(jax.random.fold_in(key_list[8], part), 9)
    rhs = gaussian(part_keys[0], (2, COMP, NPT, NQ), 2.0, 12.0, ((2, 16),), jnp.float32)
    inv_diag = draw_inv_diag(jax.random.fold_in(jax.random.fold_in(key_list[8], part), 71), part)
    face_coef = jnp.clip(0.6 + 1.1999999 * jax.random.uniform(part_keys[2], (4, NPT, NQ), jnp.float32) ** level_of(part_keys[2], (4, NPT, NQ), ((1, 16),), -0.2, 0.2), 0.6, 1.8)
    flux_jac = gaussian(key_list[3], (2, COMP, COMP), 0.3, 1.8, (), jnp.float32)
    press_weights = gaussian(key_list[4], (COMP,), 1.0, 4.0, (), jnp.float32)
    surface_cells = draw_surface_cells(jax.random.fold_in(key_list[8], 71), part)
    interface_slot = draw_interface_slot(jax.random.fold_in(key_list[8], 71), part)
    mode_shapes = bell_draw_with(key_list[7], (SURF, MODES), SURF ** -0.5, 0.09375, ((0, 16),), (0, 1, 16, 2.0), jnp.float32)
    return dict(rhs=rhs, inv_diag=inv_diag, face_coef=face_coef, flux_jac=flux_jac, press_weights=press_weights, surface_cells=surface_cells, interface_slot=interface_slot, mode_shapes=mode_shapes)


def block_apply(inv_diag, vector):
    real_part = jnp.sum(inv_diag[0] * vector[0][None], axis=1) - jnp.sum(inv_diag[1] * vector[1][None], axis=1)
    imag_part = jnp.sum(inv_diag[0] * vector[1][None], axis=1) + jnp.sum(inv_diag[1] * vector[0][None], axis=1)
    return jnp.stack([real_part, imag_part])


def couple(extended, face_coef, flux_jac):
    middle = extended[:, :, 1:-1, :]
    along_planes = face_coef[0] * extended[:, :, 2:, :] + face_coef[1] * extended[:, :, :-2, :]
    padded = jnp.pad(middle, ((0, 0), (0, 0), (0, 0), (1, 1)))
    along_cells = face_coef[2] * padded[..., 2:] + face_coef[3] * padded[..., :-2]
    mixed = jnp.einsum('kj,rjpq->rkpq', flux_jac[0], along_planes, precision=lax.Precision.HIGHEST)
    return mixed + jnp.einsum('kj,rjpq->rkpq', flux_jac[1], along_cells, precision=lax.Precision.HIGHEST)


def sweep(extended, inv_diag, rhs, face_coef, flux_jac):
    return block_apply(inv_diag, rhs + couple(extended, face_coef, flux_jac))


def reference(rhs, inv_diag, face_coef, flux_jac, press_weights, surface_cells, interface_slot, mode_shapes):
    state = block_apply(inv_diag, rhs)
    for sweep_index in range(ITERS):
        padded = jnp.pad(state, ((0, 0), (0, 0), (1, 1), (0, 0)))
        state = sweep(padded, inv_diag, rhs, face_coef, flux_jac)
    cells = state.reshape(2, COMP, N_SPACE, NP * NQ)
    pressure = jnp.sum(press_weights[None, :, None, None] * cells, axis=1)
    picks = surface_cells.reshape(N_SPACE, SD)
    surface = jnp.take_along_axis(pressure, picks[None], axis=2)
    placed = jnp.zeros((2, SURF), jnp.float32).at[:, interface_slot].set(surface.reshape(2, SURF))
    forces = jnp.dot(placed, mode_shapes, precision=lax.Precision.HIGHEST, preferred_element_type=jnp.float32)
    return state, forces
```

```python
import functools

import jax
import jax.numpy as jnp
from jax import lax
from jax.experimental import pallas as pl
from jax.experimental.pallas import tpu as pltpu
from jax.sharding import PartitionSpec as P

ITERS = 8
LANES = 128
COMP = 5
MESH = pl.DeviceIdType.MESH


def log2(value):
    assert value & (value - 1) == 0
    return value.bit_length() - 1


def thirds(x):
    a = x.astype(jnp.bfloat16)
    rest = x - a.astype(jnp.float32)
    b = rest.astype(jnp.bfloat16)
    c = (rest - b.astype(jnp.float32)).astype(jnp.bfloat16)
    return jnp.concatenate([a, b, c], axis=0)


def dot_exact(x, onehot, dims):
    rows = x.shape[0]
    out = lax.dot_general(thirds(x), onehot, (dims, ((), ())), preferred_element_type=jnp.float32)
    return (out[:rows] + out[rows : 2 * rows]) + out[2 * rows :]


def kernel(
    n, flux, press, rhs, inv, face, cells, slots, modes, state_out, forces_out,
    held, mixed, masked, send, halo, pressure, tiles, landed, part, parts,
    halo_send, halo_recv, tile_send, tile_recv, part_send, part_recv,
):
    planes, width = rhs.shape[2], rhs.shape[3]
    chunks = width // LANES
    rows = cells.shape[1]
    me = lax.axis_index("space")
    has_low, has_high = me > 0, me < n - 1

    barrier = pltpu.get_barrier_semaphore()

    def greet(d, carry):
        pl.semaphore_signal(
            barrier, inc=1, device_id={"space": lax.rem(me + d, n)}, device_id_type=MESH
        )
        return carry

    lax.fori_loop(1, n, greet, 0)

    row = lax.broadcasted_iota(jnp.int32, (planes, LANES), 0)
    lane = lax.broadcasted_iota(jnp.int32, (planes, LANES), 1)

    def at(c):
        return pl.ds(pl.multiple_of(c * LANES, LANES), LANES)

    def block_apply(c, z):
        out = []
        for k in range(COMP):
            real = imag = None
            for j in range(COMP):
                br, bi = inv[0, k, j, :, at(c)], inv[1, k, j, :, at(c)]
                re = br * z[j] - bi * z[COMP + j]
                im = br * z[COMP + j] + bi * z[j]
                real = re if real is None else real + re
                imag = im if imag is None else imag + im
            out.append((real, imag))
        return [o[0] for o in out] + [o[1] for o in out]

    def keep(c, sweep, values):
        for f in range(2 * COMP):
            held[c + 1, f] = values[f]
            send[sweep, 0, c, f] = values[f][planes - 1 :]
            send[sweep, 1, c, f] = values[f][:1]

    def first(c, carry):
        f0, f1 = face[0, :, at(c)], face[1, :, at(c)]
        zero = jnp.zeros_like(f0)
        masked[0, c] = jnp.where(row == planes - 1, zero, f0)
        masked[1, c] = jnp.where(row == 0, zero, f1)
        masked[2, c] = jnp.where(row == planes - 1, f0, zero)
        masked[3, c] = jnp.where(row == 0, f1, zero)
        z = [rhs[r, j, :, at(c)] for r in range(2) for j in range(COMP)]
        keep(c, 0, block_apply(c, z))
        return carry

    held[0] = jnp.zeros(held.shape[1:], jnp.float32)
    held[chunks + 1] = jnp.zeros(held.shape[1:], jnp.float32)

    @pl.when(jnp.logical_not(has_low))
    def _():
        for i in range(ITERS):
            halo[i, 0] = jnp.zeros(halo.shape[2:], jnp.float32)

    @pl.when(jnp.logical_not(has_high))
    def _():
        for i in range(ITERS):
            halo[i, 1] = jnp.zeros(halo.shape[2:], jnp.float32)

    lax.fori_loop(0, chunks, first, 0)
    pl.semaphore_wait(barrier, n - 1)

    def up(k):
        return pltpu.make_async_remote_copy(
            src_ref=send.at[k, 0], dst_ref=halo.at[k, 0],
            send_sem=halo_send.at[k, 0], recv_sem=halo_recv.at[k, 0],
            device_id={"space": me + 1}, device_id_type=MESH,
        )

    def down(k):
        return pltpu.make_async_remote_copy(
            src_ref=send.at[k, 1], dst_ref=halo.at[k, 1],
            send_sem=halo_send.at[k, 1], recv_sem=halo_recv.at[k, 1],
            device_id={"space": me - 1}, device_id_type=MESH,
        )

    def before(c, carry):
        f0, f1 = masked[0, c], masked[1, c]
        f2, f3 = face[2, :, at(c)], face[3, :, at(c)]
        for r in range(2):
            planewise, cellwise = [], []
            for j in range(COMP):
                f = r * COMP + j
                own = held[c + 1, f]
                after = pltpu.roll(jnp.where(lane == 0, held[c + 2, f], own), LANES - 1, 1)
                ahead = pltpu.roll(jnp.where(lane == LANES - 1, held[c, f], own), 1, 1)
                cellwise.append(f2 * after + f3 * ahead)
                planewise.append(f0 * pltpu.roll(own, planes - 1, 0) + f1 * pltpu.roll(own, 1, 0))
            for k in range(COMP):
                total = rhs[r, k, :, at(c)]
                for j in range(COMP):
                    total += flux[0, k, j] * planewise[j] + flux[1, k, j] * cellwise[j]
                mixed[c, r * COMP + k] = total
        return carry

    def sweep(s, carry):
        @pl.when(has_high)
        def _():
            up(s).start()

        @pl.when(has_low)
        def _():
            down(s).start()

        lax.fori_loop(0, chunks, before, 0)

        @pl.when(has_low)
        def _():
            up(s).wait_recv()
            down(s).wait_send()

        @pl.when(has_high)
        def _():
            down(s).wait_recv()
            up(s).wait_send()

        def behind(c, inner):
            e0, e1 = masked[2, c], masked[3, c]
            z = []
            for r in range(2):
                edge = [
                    e1 * halo[s, 0, c, r * COMP + j] + e0 * halo[s, 1, c, r * COMP + j]
                    for j in range(COMP)
                ]
                for k in range(COMP):
                    total = mixed[c, r * COMP + k]
                    for j in range(COMP):
                        total += flux[0, k, j] * edge[j]
                    z.append(total)
            keep(c, s + 1, block_apply(c, z))
            return inner

        lax.fori_loop(0, chunks, behind, 0)
        return carry

    lax.fori_loop(0, ITERS, sweep, 0)

    def finish(c, carry):
        for r in range(2):
            total = None
            for j in range(COMP):
                value = held[c + 1, r * COMP + j]
                state_out[r, j, :, at(c)] = value
                term = press[j] * value
                total = term if total is None else total + term
            pressure[r, c] = total
        return carry

    lax.fori_loop(0, chunks, finish, 0)

    cell = cells[...]
    grid = chunks * planes
    column = cell & (LANES - 1)
    place = ((cell & (width - 1)) >> log2(LANES)) * planes + (cell >> log2(width))
    pick = jnp.where(
        lax.broadcasted_iota(jnp.int32, (LANES, rows), 0) == column, 1.0, 0.0
    ).astype(jnp.bfloat16)
    flat = pressure[...].reshape(2 * grid, LANES)
    spread = dot_exact(flat, pick, ((1,), (0,)))
    here = lax.broadcasted_iota(jnp.int32, (grid, rows), 0) == place
    surface = [
        jnp.sum(jnp.where(here, spread[r * grid : (r + 1) * grid], 0.0), axis=0, keepdims=True)
        for r in range(2)
    ]

    slot = slots[...]
    deep = rows // LANES
    tall = 2 * deep
    index = lax.broadcasted_iota(jnp.int32, (n * tall, rows), 0)
    wanted = (index >> log2(tall)) * deep + (index & (deep - 1))
    value = jnp.where((index & (tall - 1)) < deep, surface[0], surface[1])
    value = jnp.where(wanted == (slot >> log2(LANES)), value, 0.0)
    put = jnp.where(
        lax.broadcasted_iota(jnp.int32, (LANES, rows), 0) == (slot & (LANES - 1)), 1.0, 0.0
    ).astype(jnp.bfloat16)
    tiles[...] = dot_exact(value, put, ((1,), (1,))).reshape(n, tall, LANES)

    def tile_copy(d):
        target = lax.rem(me + d, n)
        return pltpu.make_async_remote_copy(
            src_ref=tiles.at[target], dst_ref=landed.at[d],
            send_sem=tile_send.at[d], recv_sem=tile_recv.at[d],
            device_id={"space": target}, device_id_type=MESH,
        )

    def part_copy(d):
        return pltpu.make_async_remote_copy(
            src_ref=part, dst_ref=parts.at[d],
            send_sem=part_send.at[d], recv_sem=part_recv.at[d],
            device_id={"space": lax.rem(me + d, n)}, device_id_type=MESH,
        )

    def run(copy):
        def start(d, carry):
            copy(d).start()
            return carry

        def wait(d, carry):
            copy(d).wait()
            return carry

        lax.fori_loop(1, n, start, 0)
        lax.fori_loop(1, n, wait, 0)

    landed[0] = tiles[me]
    run(tile_copy)
    placed = jnp.sum(landed[...], axis=0)
    share = [None, None]
    for j in range(deep):
        product = jnp.dot(
            placed, modes[j * LANES : (j + 1) * LANES, :],
            precision=lax.Precision.HIGHEST, preferred_element_type=jnp.float32,
        )
        for r in range(2):
            term = product[r * deep + j : r * deep + j + 1]
            share[r] = term if share[r] is None else share[r] + term
    count = modes.shape[1]
    part[...] = jnp.zeros(part.shape, jnp.float32)
    for r in range(2):
        part[r : r + 1, :count] = share[r]
    parts[0] = part[...]
    run(part_copy)
    total = jnp.sum(parts[...], axis=0)[:, :count]
    mine = forces_out.shape[1]
    choose = (
        lax.broadcasted_iota(jnp.int32, (count, mine), 0)
        == lax.broadcasted_iota(jnp.int32, (count, mine), 1) + me * mine
    )
    forces_out[...] = dot_exact(
        total, jnp.where(choose, 1.0, 0.0).astype(jnp.bfloat16), ((1,), (0,))
    )[:2]


def local(
    rhs, inv_diag, face_coef, flux_jac, press_weights, surface_cells, interface_slot, mode_shapes
):
    n = lax.axis_size("space")
    planes, width = rhs.shape[2:]
    chunks = width // LANES
    rows, count = mode_shapes.shape
    tall = 2 * (rows // LANES)
    padded = -(-count // LANES) * LANES
    vmem = pl.BlockSpec(memory_space=pltpu.VMEM)
    smem = pl.BlockSpec(memory_space=pltpu.SMEM)
    f32 = jnp.float32
    dma = pltpu.SemaphoreType.DMA
    return pl.pallas_call(
        functools.partial(kernel, n),
        out_shape=(
            jax.ShapeDtypeStruct(rhs.shape, f32),
            jax.ShapeDtypeStruct((2, count // n), f32),
        ),
        in_specs=[smem, smem] + [vmem] * 6,
        out_specs=(vmem, vmem),
        scratch_shapes=[
            pltpu.VMEM((chunks + 2, 2 * COMP, planes, LANES), f32),
            pltpu.VMEM((chunks, 2 * COMP, planes, LANES), f32),
            pltpu.VMEM((4, chunks, planes, LANES), f32),
            pltpu.VMEM((ITERS + 1, 2, chunks, 2 * COMP, 1, LANES), f32),
            pltpu.VMEM((ITERS, 2, chunks, 2 * COMP, 1, LANES), f32),
            pltpu.VMEM((2, chunks, planes, LANES), f32),
            pltpu.VMEM((n, tall, LANES), f32),
            pltpu.VMEM((n, tall, LANES), f32),
            pltpu.VMEM((8, padded), f32),
            pltpu.VMEM((n, 8, padded), f32),
            dma((ITERS, 2)), dma((ITERS, 2)), dma((n,)), dma((n,)), dma((n,)), dma((n,)),
        ],
        compiler_params=pltpu.CompilerParams(
            collective_id=0, has_side_effects=True, vmem_limit_bytes=40 * 2**20
        ),
    )(
        flux_jac, press_weights, rhs, inv_diag, face_coef,
        surface_cells.reshape(1, rows), interface_slot.reshape(1, rows), mode_shapes,
    )


def solution(mesh):
    in_specs = (
        P(None, None, ("freq", "space"), None),
        P(None, None, None, ("freq", "space"), None),
        P(None, ("freq", "space"), None),
        P(),
        P(),
        P("space"),
        P("space"),
        P("space", None),
    )
    out_specs = (P(None, None, ("freq", "space"), None), P(None, ("freq", "space")))
    return jax.shard_map(local, mesh=mesh, in_specs=in_specs, out_specs=out_specs, check_vma=False)
```

```python
import functools

import jax
import jax.numpy as jnp
from jax import lax
from jax.experimental import pallas as pl
from jax.experimental.pallas import tpu as pltpu
from jax.sharding import PartitionSpec as P

ITERS = 8
LANES = 128
COMP = 5
MESH = pl.DeviceIdType.MESH


def log2(value):
    assert value & (value - 1) == 0
    return value.bit_length() - 1


def thirds(x):
    a = x.astype(jnp.bfloat16)
    rest = x - a.astype(jnp.float32)
    b = rest.astype(jnp.bfloat16)
    c = (rest - b.astype(jnp.float32)).astype(jnp.bfloat16)
    return jnp.concatenate([a, b, c], axis=0)


def dot_exact(x, onehot, dims):
    rows = x.shape[0]
    out = lax.dot_general(thirds(x), onehot, (dims, ((), ())), preferred_element_type=jnp.float32)
    return (out[:rows] + out[rows : 2 * rows]) + out[2 * rows :]


def kernel(
    n, flux, press, rhs_in, inv_in, face_in, cells_in, slots_in, modes_in, state_out, forces_out,
    rhs, inv, face, cells, slots, modes, loaded,
    held, mixed, masked, send, halo, fixed, beside, outer, pick, here, wanted, put,
    pressure, tiles, landed, part, parts,
    halo_send, halo_recv, fixed_send, fixed_recv,
    tile_send, tile_recv, part_send, part_recv,
):
    loads = [
        pltpu.make_async_copy(src, dst, loaded.at[i])
        for i, (src, dst) in enumerate(
            (
                (rhs_in, rhs), (inv_in, inv), (face_in, face),
                (cells_in, cells), (slots_in, slots), (modes_in, modes),
            )
        )
    ]
    for load in loads:
        load.start()
    planes, width = rhs.shape[2], rhs.shape[3]
    chunks = width // LANES
    rows = cells.shape[1]
    me = lax.axis_index("space")
    has_low, has_high = me > 0, me < n - 1

    barrier = pltpu.get_barrier_semaphore()

    def greet(d, carry):
        pl.semaphore_signal(
            barrier, inc=1, device_id={"space": lax.rem(me + d, n)}, device_id_type=MESH
        )
        return carry

    lax.fori_loop(1, n, greet, 0)

    row = lax.broadcasted_iota(jnp.int32, (planes, LANES), 0)
    lane = lax.broadcasted_iota(jnp.int32, (planes, LANES), 1)

    def at(c):
        return pl.ds(pl.multiple_of(c * LANES, LANES), LANES)

    def block_apply(block, z):
        reals, imags = [], []
        for k in range(COMP):
            real = imag = None
            for j in range(COMP):
                br, bi = block(k * COMP + j), block((COMP + k) * COMP + j)
                re = br * z[j] - bi * z[COMP + j]
                im = br * z[COMP + j] + bi * z[j]
                real = re if real is None else real + re
                imag = im if imag is None else imag + im
            reals.append(real)
            imags.append(imag)
        return reals + imags

    def own_block(c):
        return lambda i: inv[i // (COMP * COMP), i // COMP % COMP, i % COMP, :, at(c)]

    def keep(c, exchange, values):
        for f in range(2 * COMP):
            held[c + 1, f] = values[f]
            if exchange is not None:
                for p in range(2):
                    send[exchange, 0, p, f, pl.ds(c, 1)] = values[f][planes - 1 - p : planes - p]
                    send[exchange, 1, p, f, pl.ds(c, 1)] = values[f][p : p + 1]

    fields = 2 * COMP * COMP

    def first(c, carry):
        f0, f1 = face[0, :, at(c)], face[1, :, at(c)]
        zero = jnp.zeros_like(f0)
        masked[0, c] = jnp.where(row == planes - 1, zero, f0)
        masked[1, c] = jnp.where(row == 0, zero, f1)
        masked[2, c] = jnp.where(row == planes - 1, f0, zero)
        masked[3, c] = jnp.where(row == 0, f1, zero)
        z = [rhs[r, j, :, at(c)] for r in range(2) for j in range(COMP)]
        keep(c, 0, block_apply(own_block(c), z))
        block = own_block(c)
        f2, f3 = face[2, :, at(c)], face[3, :, at(c)]
        for i, x in enumerate([block(i) for i in range(fields)] + z):
            fixed[0, i, pl.ds(c, 1)] = x[planes - 1 :]
            fixed[1, i, pl.ds(c, 1)] = x[:1]
        for i, (x, y) in enumerate(((f0, f1), (f1, f0), (f2, f2), (f3, f3))):
            fixed[0, fields + 2 * COMP + i, pl.ds(c, 1)] = x[planes - 1 :]
            fixed[1, fields + 2 * COMP + i, pl.ds(c, 1)] = y[:1]
        return carry

    held[0] = jnp.zeros(held.shape[1:], jnp.float32)
    held[chunks + 1] = jnp.zeros(held.shape[1:], jnp.float32)

    @pl.when(jnp.logical_not(has_low))
    def _():
        beside[0] = jnp.zeros(beside.shape[1:], jnp.float32)
        for i in range(ITERS // 2):
            halo[i, 0] = jnp.zeros(halo.shape[2:], jnp.float32)

    @pl.when(jnp.logical_not(has_high))
    def _():
        beside[1] = jnp.zeros(beside.shape[1:], jnp.float32)
        for i in range(ITERS // 2):
            halo[i, 1] = jnp.zeros(halo.shape[2:], jnp.float32)

    for load in loads[:3]:
        load.wait()
    lax.fori_loop(0, chunks, first, 0)
    pl.semaphore_wait(barrier, n - 1)

    def state_copy(k, side):
        return pltpu.make_async_remote_copy(
            src_ref=send.at[k, side], dst_ref=halo.at[k, side],
            send_sem=halo_send.at[k, side], recv_sem=halo_recv.at[k, side],
            device_id={"space": me + 1 - 2 * side}, device_id_type=MESH,
        )

    def fixed_copy(side):
        return pltpu.make_async_remote_copy(
            src_ref=fixed.at[side], dst_ref=beside.at[side],
            send_sem=fixed_send.at[side], recv_sem=fixed_recv.at[side],
            device_id={"space": me + 1 - 2 * side}, device_id_type=MESH,
        )

    def exchange(k):
        for side, there in ((0, has_high), (1, has_low)):
            pl.when(there)(state_copy(k, side).start)

    exchange(0)
    for side, there in ((0, has_high), (1, has_low)):
        pl.when(there)(fixed_copy(side).start)

    def before(c, carry):
        f0, f1 = masked[0, c], masked[1, c]
        f2, f3 = face[2, :, at(c)], face[3, :, at(c)]
        for r in range(2):
            planewise, cellwise = [], []
            for j in range(COMP):
                f = r * COMP + j
                own = held[c + 1, f]
                after = pltpu.roll(jnp.where(lane == 0, held[c + 2, f], own), LANES - 1, 1)
                ahead = pltpu.roll(jnp.where(lane == LANES - 1, held[c, f], own), 1, 1)
                cellwise.append(f2 * after + f3 * ahead)
                planewise.append(f0 * pltpu.roll(own, planes - 1, 0) + f1 * pltpu.roll(own, 1, 0))
            for k in range(COMP):
                total = rhs[r, k, :, at(c)]
                for j in range(COMP):
                    total += flux[k, 0, j] * planewise[j] + flux[k, 1, j] * cellwise[j]
                mixed[c, r * COMP + k] = total
        return carry

    def behind(c, low, high, exchange):
        e0, e1 = masked[2, c], masked[3, c]
        z = []
        for r in range(2):
            edge = [e1 * low(r * COMP + j, c) + e0 * high(r * COMP + j, c) for j in range(COMP)]
            for k in range(COMP):
                total = mixed[c, r * COMP + k]
                for j in range(COMP):
                    total += flux[k, 0, j] * edge[j]
                z.append(total)
        keep(c, exchange, block_apply(own_block(c), z))

    chunk_row = lax.broadcasted_iota(jnp.int32, (chunks, LANES), 0)
    chunk_lane = lax.broadcasted_iota(jnp.int32, (chunks, LANES), 1)
    first_cell = (chunk_row == 0) & (chunk_lane == 0)
    last_cell = (chunk_row == chunks - 1) & (chunk_lane == LANES - 1)

    def sweep_outer(s, side):
        coefs = [beside[side, fields + 2 * COMP + i] for i in range(4)]
        z = []
        for r in range(2):
            planewise, cellwise = [], []
            for j in range(COMP):
                f = r * COMP + j
                x = halo[s, side, 0, f]
                after = pltpu.roll(
                    jnp.where(chunk_lane == 0, pltpu.roll(x, chunks - 1, 0), x), LANES - 1, 1
                )
                ahead = pltpu.roll(
                    jnp.where(chunk_lane == LANES - 1, pltpu.roll(x, 1, 0), x), 1, 1
                )
                cellwise.append(
                    coefs[2] * jnp.where(last_cell, 0.0, after)
                    + coefs[3] * jnp.where(first_cell, 0.0, ahead)
                )
                planewise.append(
                    coefs[0] * send[s, 1 - side, 0, f] + coefs[1] * halo[s, side, 1, f]
                )
            for k in range(COMP):
                total = beside[side, fields + r * COMP + k]
                for j in range(COMP):
                    total += flux[k, 0, j] * planewise[j] + flux[k, 1, j] * cellwise[j]
                z.append(total)
        values = block_apply(lambda i: beside[side, i], z)
        for f in range(2 * COMP):
            outer[side, f] = values[f]

    def two_sweeps(s, carry):
        lax.fori_loop(0, chunks, before, 0)
        for there, come, gone in ((has_low, 0, 1), (has_high, 1, 0)):
            @pl.when(there)
            def _():
                state_copy(s, come).wait_recv()
                state_copy(s, gone).wait_send()

            @pl.when(there & (s == 0))
            def _():
                fixed_copy(come).wait_recv()
                fixed_copy(gone).wait_send()

        def with_halo(c, inner):
            behind(
                c,
                lambda f, c: halo[s, 0, 0, f, pl.ds(c, 1)],
                lambda f, c: halo[s, 1, 0, f, pl.ds(c, 1)],
                None,
            )
            return inner

        lax.fori_loop(0, chunks, with_halo, 0)
        for side in range(2):
            sweep_outer(s, side)
        lax.fori_loop(0, chunks, before, 0)

        def with_outer(c, inner):
            behind(
                c,
                lambda f, c: outer[0, f, pl.ds(c, 1)],
                lambda f, c: outer[1, f, pl.ds(c, 1)],
                s + 1,
            )
            return inner

        lax.fori_loop(0, chunks, with_outer, 0)
        pl.when(s + 1 < ITERS // 2)(lambda: exchange(s + 1))
        return carry

    for load in loads[3:]:
        load.wait()
    cell, slot = cells[...], slots[...]
    grid = chunks * planes
    place = ((cell & (width - 1)) >> log2(LANES)) * planes + (cell >> log2(width))
    deep = rows // LANES
    tall = 2 * deep

    def count_rows(size):
        return lax.broadcasted_iota(jnp.int32, (size, rows), 0)

    def ones(where):
        return jnp.where(where, 1.0, 0.0)

    pick[...] = ones(count_rows(LANES) == (cell & (LANES - 1))).astype(jnp.bfloat16)
    put[...] = ones(count_rows(LANES) == (slot & (LANES - 1))).astype(jnp.bfloat16)
    here[...] = ones(count_rows(grid) == place)
    index = count_rows(n * tall)
    wanted[...] = ones(
        (index >> log2(tall)) * deep + (index & (deep - 1)) == (slot >> log2(LANES))
    )

    lax.fori_loop(0, ITERS // 2, two_sweeps, 0)

    def finish(c, carry):
        for r in range(2):
            total = None
            for j in range(COMP):
                value = held[c + 1, r * COMP + j]
                state_out[r, j, :, at(c)] = value
                term = press[j] * value
                total = term if total is None else total + term
            pressure[r, c] = total
        return carry

    lax.fori_loop(0, chunks, finish, 0)

    spread = dot_exact(pressure[...].reshape(2 * grid, LANES), pick[...], ((1,), (0,)))
    surface = [
        jnp.sum(here[...] * spread[r * grid : (r + 1) * grid], axis=0, keepdims=True)
        for r in range(2)
    ]
    value = wanted[...] * jnp.where(
        (count_rows(n * tall) & (tall - 1)) < deep, surface[0], surface[1]
    )
    tiles[...] = dot_exact(value, put[...], ((1,), (1,))).reshape(n, tall, LANES)

    def tile_copy(d):
        target = lax.rem(me + d, n)
        return pltpu.make_async_remote_copy(
            src_ref=tiles.at[target], dst_ref=landed.at[d],
            send_sem=tile_send.at[d], recv_sem=tile_recv.at[d],
            device_id={"space": target}, device_id_type=MESH,
        )

    def part_copy(d):
        return pltpu.make_async_remote_copy(
            src_ref=part, dst_ref=parts.at[d],
            send_sem=part_send.at[d], recv_sem=part_recv.at[d],
            device_id={"space": lax.rem(me + d, n)}, device_id_type=MESH,
        )

    def run(copy):
        def start(d, carry):
            copy(d).start()
            return carry

        def wait(d, carry):
            copy(d).wait()
            return carry

        lax.fori_loop(1, n, start, 0)
        lax.fori_loop(1, n, wait, 0)

    landed[0] = tiles[me]
    run(tile_copy)
    placed = jnp.sum(landed[...], axis=0)
    share = [None, None]
    for j in range(deep):
        product = lax.dot_general(
            placed, modes[:, j * LANES : (j + 1) * LANES], (((1,), (1,)), ((), ())),
            precision=lax.Precision.HIGHEST, preferred_element_type=jnp.float32,
        )
        for r in range(2):
            term = product[r * deep + j : r * deep + j + 1]
            share[r] = term if share[r] is None else share[r] + term
    count = modes.shape[0]
    part[...] = jnp.zeros(part.shape, jnp.float32)
    for r in range(2):
        part[r : r + 1, :count] = share[r]
    parts[0] = part[...]
    run(part_copy)
    total = jnp.sum(parts[...], axis=0)[:, :count]
    mine = forces_out.shape[1]
    choose = (
        lax.broadcasted_iota(jnp.int32, (count, mine), 0)
        == lax.broadcasted_iota(jnp.int32, (count, mine), 1) + me * mine
    )
    forces_out[...] = dot_exact(
        total, jnp.where(choose, 1.0, 0.0).astype(jnp.bfloat16), ((1,), (0,))
    )


def local(
    rhs, inv_diag, face_coef, flux_jac, press_weights, surface_cells, interface_slot, mode_shapes
):
    n = lax.axis_size("space")
    planes, width = rhs.shape[2:]
    chunks = width // LANES
    rows, count = mode_shapes.shape
    tall = 2 * (rows // LANES)
    padded = -(-count // LANES) * LANES
    vmem = pl.BlockSpec(memory_space=pltpu.VMEM)
    hbm = pl.BlockSpec(memory_space=pltpu.HBM)
    smem = pl.BlockSpec(memory_space=pltpu.SMEM)
    f32 = jnp.float32
    dma = pltpu.SemaphoreType.DMA
    return pl.pallas_call(
        functools.partial(kernel, n),
        out_shape=(
            jax.ShapeDtypeStruct(rhs.shape, f32),
            jax.ShapeDtypeStruct((2, count // n), f32),
        ),
        in_specs=[smem, smem] + [hbm] * 6,
        out_specs=(vmem, vmem),
        scratch_shapes=[
            pltpu.VMEM(rhs.shape, f32),
            pltpu.VMEM(inv_diag.shape, f32),
            pltpu.VMEM(face_coef.shape, f32),
            pltpu.VMEM((1, rows), jnp.int32),
            pltpu.VMEM((1, rows), jnp.int32),
            pltpu.VMEM((count, rows), f32),
            dma((6,)),
            pltpu.VMEM((chunks + 2, 2 * COMP, planes, LANES), f32),
            pltpu.VMEM((chunks, 2 * COMP, planes, LANES), f32),
            pltpu.VMEM((4, chunks, planes, LANES), f32),
            pltpu.VMEM((ITERS // 2 + 1, 2, 2, 2 * COMP, chunks, LANES), f32),
            pltpu.VMEM((ITERS // 2, 2, 2, 2 * COMP, chunks, LANES), f32),
            pltpu.VMEM((2, 2 * COMP * (COMP + 1) + 4, chunks, LANES), f32),
            pltpu.VMEM((2, 2 * COMP * (COMP + 1) + 4, chunks, LANES), f32),
            pltpu.VMEM((2, 2 * COMP, chunks, LANES), f32),
            pltpu.VMEM((LANES, rows), jnp.bfloat16),
            pltpu.VMEM((chunks * planes, rows), f32),
            pltpu.VMEM((n * tall, rows), f32),
            pltpu.VMEM((LANES, rows), jnp.bfloat16),
            pltpu.VMEM((2, chunks, planes, LANES), f32),
            pltpu.VMEM((n, tall, LANES), f32),
            pltpu.VMEM((n, tall, LANES), f32),
            pltpu.VMEM((2, padded), f32),
            pltpu.VMEM((n, 2, padded), f32),
            dma((ITERS // 2, 2)), dma((ITERS // 2, 2)), dma((2,)), dma((2,)), dma((n,)), dma((n,)), dma((n,)), dma((n,)),
        ],
        compiler_params=pltpu.CompilerParams(
            collective_id=0, has_side_effects=True, vmem_limit_bytes=63 * 2**20
        ),
    )(
        flux_jac.transpose(1, 0, 2), press_weights, rhs, inv_diag, face_coef,
        surface_cells.reshape(1, rows), interface_slot.reshape(1, rows), mode_shapes.T,
    )


def solution(mesh):
    in_specs = (
        P(None, None, ("freq", "space"), None),
        P(None, None, None, ("freq", "space"), None),
        P(None, ("freq", "space"), None),
        P(),
        P(),
        P("space"),
        P("space"),
        P("space", None),
    )
    out_specs = (P(None, None, ("freq", "space"), None), P(None, ("freq", "space")))
    return jax.shard_map(local, mesh=mesh, in_specs=in_specs, out_specs=out_specs, check_vma=False)
```

```python
import functools

import jax
import jax.numpy as jnp
from jax import lax
from jax.experimental import pallas as pl
from jax.experimental.pallas import tpu as pltpu
from jax.sharding import PartitionSpec as P

ITERS = 8
UNROLL = 4
LANES = 128
COMP = 5
MESH = pl.DeviceIdType.MESH


def log2(value):
    assert value & (value - 1) == 0
    return value.bit_length() - 1


def thirds(x):
    a = x.astype(jnp.bfloat16)
    rest = x - a.astype(jnp.float32)
    b = rest.astype(jnp.bfloat16)
    c = (rest - b.astype(jnp.float32)).astype(jnp.bfloat16)
    return jnp.concatenate([a, b, c], axis=0)


def dot_exact(x, onehot, dims):
    rows = x.shape[0]
    out = lax.dot_general(thirds(x), onehot, (dims, ((), ())), preferred_element_type=jnp.float32)
    return (out[:rows] + out[rows : 2 * rows]) + out[2 * rows :]


def kernel(
    n, flux, press, rhs_in, inv_in, face_in, cells_in, slots_in, modes_in, state_out, forces_out,
    rhs, inv, face, cells, slots, modes, loaded,
    held, mixed, masked, send, halo, fixed, beside, outer, pick, here, wanted, put,
    pressure, tiles, landed, part, parts,
    halo_send, halo_recv, fixed_send, fixed_recv,
    tile_send, tile_recv, part_send, part_recv,
):
    loads = [
        pltpu.make_async_copy(src, dst, loaded.at[i])
        for i, (src, dst) in enumerate(
            (
                (rhs_in, rhs), (inv_in, inv), (face_in, face),
                (cells_in, cells), (slots_in, slots), (modes_in, modes),
            )
        )
    ]
    for load in loads:
        load.start()
    planes, width = rhs.shape[2], rhs.shape[3]
    chunks = width // LANES
    rows = cells.shape[1]
    me = lax.axis_index("space")
    has_low, has_high = me > 0, me < n - 1

    barrier = pltpu.get_barrier_semaphore()

    def greet(d, carry):
        pl.semaphore_signal(
            barrier, inc=1, device_id={"space": lax.rem(me + d, n)}, device_id_type=MESH
        )
        return carry

    lax.fori_loop(1, n, greet, 0, unroll=True)

    row = lax.broadcasted_iota(jnp.int32, (planes, LANES), 0)
    lane = lax.broadcasted_iota(jnp.int32, (planes, LANES), 1)

    def at(c):
        return pl.ds(pl.multiple_of(c * LANES, LANES), LANES)

    def block_apply(block, z):
        reals, imags = [], []
        for k in range(COMP):
            real = imag = None
            for j in range(COMP):
                br, bi = block(k * COMP + j), block((COMP + k) * COMP + j)
                re = br * z[j] - bi * z[COMP + j]
                im = br * z[COMP + j] + bi * z[j]
                real = re if real is None else real + re
                imag = im if imag is None else imag + im
            reals.append(real)
            imags.append(imag)
        return reals + imags

    def own_block(c):
        return lambda i: inv[i // (COMP * COMP), i // COMP % COMP, i % COMP, :, at(c)]

    def keep(c, exchange, values):
        for f in range(2 * COMP):
            held[c + 1, f] = values[f]
            if exchange is not None:
                for p in range(2):
                    send[exchange, 0, p, f, pl.ds(c, 1)] = values[f][planes - 1 - p : planes - p]
                    send[exchange, 1, p, f, pl.ds(c, 1)] = values[f][p : p + 1]

    fields = 2 * COMP * COMP

    def first(c, carry):
        f0, f1 = face[0, :, at(c)], face[1, :, at(c)]
        zero = jnp.zeros_like(f0)
        masked[0, c] = jnp.where(row == planes - 1, zero, f0)
        masked[1, c] = jnp.where(row == 0, zero, f1)
        masked[2, c] = jnp.where(row == planes - 1, f0, zero)
        masked[3, c] = jnp.where(row == 0, f1, zero)
        z = [rhs[r, j, :, at(c)] for r in range(2) for j in range(COMP)]
        keep(c, 0, block_apply(own_block(c), z))
        block = own_block(c)
        f2, f3 = face[2, :, at(c)], face[3, :, at(c)]
        for i, x in enumerate([block(i) for i in range(fields)] + z):
            fixed[0, i, pl.ds(c, 1)] = x[planes - 1 :]
            fixed[1, i, pl.ds(c, 1)] = x[:1]
        for i, (x, y) in enumerate(((f0, f1), (f1, f0), (f2, f2), (f3, f3))):
            fixed[0, fields + 2 * COMP + i, pl.ds(c, 1)] = x[planes - 1 :]
            fixed[1, fields + 2 * COMP + i, pl.ds(c, 1)] = y[:1]
        return carry

    held[0] = jnp.zeros(held.shape[1:], jnp.float32)
    held[chunks + 1] = jnp.zeros(held.shape[1:], jnp.float32)

    @pl.when(jnp.logical_not(has_low))
    def _():
        beside[0] = jnp.zeros(beside.shape[1:], jnp.float32)
        for i in range(ITERS // 2):
            halo[i, 0] = jnp.zeros(halo.shape[2:], jnp.float32)

    @pl.when(jnp.logical_not(has_high))
    def _():
        beside[1] = jnp.zeros(beside.shape[1:], jnp.float32)
        for i in range(ITERS // 2):
            halo[i, 1] = jnp.zeros(halo.shape[2:], jnp.float32)

    for load in loads[:3]:
        load.wait()
    lax.fori_loop(0, chunks, first, 0, unroll=UNROLL)
    pl.semaphore_wait(barrier, n - 1)

    def state_copy(k, side):
        return pltpu.make_async_remote_copy(
            src_ref=send.at[k, side], dst_ref=halo.at[k, side],
            send_sem=halo_send.at[k, side], recv_sem=halo_recv.at[k, side],
            device_id={"space": me + 1 - 2 * side}, device_id_type=MESH,
        )

    def fixed_copy(side):
        return pltpu.make_async_remote_copy(
            src_ref=fixed.at[side], dst_ref=beside.at[side],
            send_sem=fixed_send.at[side], recv_sem=fixed_recv.at[side],
            device_id={"space": me + 1 - 2 * side}, device_id_type=MESH,
        )

    def exchange(k):
        for side, there in ((0, has_high), (1, has_low)):
            pl.when(there)(state_copy(k, side).start)

    exchange(0)
    for side, there in ((0, has_high), (1, has_low)):
        pl.when(there)(fixed_copy(side).start)

    def before(c, carry):
        f0, f1 = masked[0, c], masked[1, c]
        f2, f3 = face[2, :, at(c)], face[3, :, at(c)]
        for r in range(2):
            planewise, cellwise = [], []
            for j in range(COMP):
                f = r * COMP + j
                own = held[c + 1, f]
                after = pltpu.roll(jnp.where(lane == 0, held[c + 2, f], own), LANES - 1, 1)
                ahead = pltpu.roll(jnp.where(lane == LANES - 1, held[c, f], own), 1, 1)
                cellwise.append(f2 * after + f3 * ahead)
                planewise.append(f0 * pltpu.roll(own, planes - 1, 0) + f1 * pltpu.roll(own, 1, 0))
            for k in range(COMP):
                total = rhs[r, k, :, at(c)]
                for j in range(COMP):
                    total += flux[k, 0, j] * planewise[j] + flux[k, 1, j] * cellwise[j]
                mixed[c, r * COMP + k] = total
        return carry

    def behind(c, low, high, exchange):
        e0, e1 = masked[2, c], masked[3, c]
        z = []
        for r in range(2):
            edge = [e1 * low(r * COMP + j, c) + e0 * high(r * COMP + j, c) for j in range(COMP)]
            for k in range(COMP):
                total = mixed[c, r * COMP + k]
                for j in range(COMP):
                    total += flux[k, 0, j] * edge[j]
                z.append(total)
        keep(c, exchange, block_apply(own_block(c), z))

    chunk_row = lax.broadcasted_iota(jnp.int32, (chunks, LANES), 0)
    chunk_lane = lax.broadcasted_iota(jnp.int32, (chunks, LANES), 1)
    first_cell = (chunk_row == 0) & (chunk_lane == 0)
    last_cell = (chunk_row == chunks - 1) & (chunk_lane == LANES - 1)

    def sweep_outer(s, side):
        coefs = [beside[side, fields + 2 * COMP + i] for i in range(4)]
        z = []
        for r in range(2):
            planewise, cellwise = [], []
            for j in range(COMP):
                f = r * COMP + j
                x = halo[s, side, 0, f]
                after = pltpu.roll(
                    jnp.where(chunk_lane == 0, pltpu.roll(x, chunks - 1, 0), x), LANES - 1, 1
                )
                ahead = pltpu.roll(
                    jnp.where(chunk_lane == LANES - 1, pltpu.roll(x, 1, 0), x), 1, 1
                )
                cellwise.append(
                    coefs[2] * jnp.where(last_cell, 0.0, after)
                    + coefs[3] * jnp.where(first_cell, 0.0, ahead)
                )
                planewise.append(
                    coefs[0] * send[s, 1 - side, 0, f] + coefs[1] * halo[s, side, 1, f]
                )
            for k in range(COMP):
                total = beside[side, fields + r * COMP + k]
                for j in range(COMP):
                    total += flux[k, 0, j] * planewise[j] + flux[k, 1, j] * cellwise[j]
                z.append(total)
        values = block_apply(lambda i: beside[side, i], z)
        for f in range(2 * COMP):
            outer[side, f] = values[f]

    def two_sweeps(s, carry):
        lax.fori_loop(0, chunks, before, 0, unroll=UNROLL)
        for there, come, gone in ((has_low, 0, 1), (has_high, 1, 0)):
            @pl.when(there)
            def _():
                state_copy(s, come).wait_recv()
                state_copy(s, gone).wait_send()

        def with_halo(c, inner):
            behind(
                c,
                lambda f, c: halo[s, 0, 0, f, pl.ds(c, 1)],
                lambda f, c: halo[s, 1, 0, f, pl.ds(c, 1)],
                None,
            )
            return inner

        lax.fori_loop(0, chunks, with_halo, 0, unroll=UNROLL)
        lax.fori_loop(0, chunks, before, 0, unroll=UNROLL)
        for there, come, gone in ((has_low, 0, 1), (has_high, 1, 0)):
            @pl.when(there & (s == 0))
            def _():
                fixed_copy(come).wait_recv()
                fixed_copy(gone).wait_send()

        for side in range(2):
            sweep_outer(s, side)

        def with_outer(c, inner):
            behind(
                c,
                lambda f, c: outer[0, f, pl.ds(c, 1)],
                lambda f, c: outer[1, f, pl.ds(c, 1)],
                s + 1,
            )
            return inner

        lax.fori_loop(0, chunks, with_outer, 0, unroll=UNROLL)
        pl.when(s + 1 < ITERS // 2)(lambda: exchange(s + 1))
        return carry

    for load in loads[3:]:
        load.wait()
    cell, slot = cells[...], slots[...]
    grid = chunks * planes
    place = ((cell & (width - 1)) >> log2(LANES)) * planes + (cell >> log2(width))
    deep = rows // LANES
    tall = 2 * deep

    def count_rows(size):
        return lax.broadcasted_iota(jnp.int32, (size, rows), 0)

    def ones(where):
        return jnp.where(where, 1.0, 0.0)

    pick[...] = ones(count_rows(LANES) == (cell & (LANES - 1))).astype(jnp.bfloat16)
    put[...] = ones(count_rows(LANES) == (slot & (LANES - 1))).astype(jnp.bfloat16)
    here[...] = ones(count_rows(grid) == place)
    index = count_rows(n * tall)
    wanted[...] = ones(
        (index >> log2(tall)) * deep + (index & (deep - 1)) == (slot >> log2(LANES))
    )

    lax.fori_loop(0, ITERS // 2, two_sweeps, 0)

    def finish(c, carry):
        for r in range(2):
            total = None
            for j in range(COMP):
                value = held[c + 1, r * COMP + j]
                state_out[r, j, :, at(c)] = value
                term = press[j] * value
                total = term if total is None else total + term
            pressure[r, c] = total
        return carry

    lax.fori_loop(0, chunks, finish, 0, unroll=UNROLL)

    spread = dot_exact(pressure[...].reshape(2 * grid, LANES), pick[...], ((1,), (0,)))
    surface = [
        jnp.sum(here[...] * spread[r * grid : (r + 1) * grid], axis=0, keepdims=True)
        for r in range(2)
    ]
    value = wanted[...] * jnp.where(
        (count_rows(n * tall) & (tall - 1)) < deep, surface[0], surface[1]
    )
    tiles[...] = dot_exact(value, put[...], ((1,), (1,))).reshape(n, tall, LANES)

    def tile_copy(d):
        target = lax.rem(me + d, n)
        return pltpu.make_async_remote_copy(
            src_ref=tiles.at[target], dst_ref=landed.at[d],
            send_sem=tile_send.at[d], recv_sem=tile_recv.at[d],
            device_id={"space": target}, device_id_type=MESH,
        )

    def part_copy(d):
        return pltpu.make_async_remote_copy(
            src_ref=part, dst_ref=parts.at[d],
            send_sem=part_send.at[d], recv_sem=part_recv.at[d],
            device_id={"space": lax.rem(me + d, n)}, device_id_type=MESH,
        )

    def run(copy):
        def start(d, carry):
            copy(d).start()
            return carry

        def wait(d, carry):
            copy(d).wait()
            return carry

        lax.fori_loop(1, n, start, 0, unroll=True)
        lax.fori_loop(1, n, wait, 0, unroll=True)

    landed[0] = tiles[me]
    run(tile_copy)
    placed = jnp.sum(landed[...], axis=0)
    share = [None, None]
    for j in range(deep):
        product = lax.dot_general(
            placed, modes[:, j * LANES : (j + 1) * LANES], (((1,), (1,)), ((), ())),
            precision=lax.Precision.HIGHEST, preferred_element_type=jnp.float32,
        )
        for r in range(2):
            term = product[r * deep + j : r * deep + j + 1]
            share[r] = term if share[r] is None else share[r] + term
    count = modes.shape[0]
    part[...] = jnp.zeros(part.shape, jnp.float32)
    for r in range(2):
        part[r : r + 1, :count] = share[r]
    parts[0] = part[...]
    run(part_copy)
    total = jnp.sum(parts[...], axis=0)[:, :count]
    mine = forces_out.shape[1]
    choose = (
        lax.broadcasted_iota(jnp.int32, (count, mine), 0)
        == lax.broadcasted_iota(jnp.int32, (count, mine), 1) + me * mine
    )
    forces_out[...] = dot_exact(
        total, jnp.where(choose, 1.0, 0.0).astype(jnp.bfloat16), ((1,), (0,))
    )


def hand_over(state, forces, state_out, forces_out, state_held, forces_held, done):
    routes = ((state, state_held, state_out), (forces, forces_held, forces_out))
    inward = [pltpu.make_async_copy(a, b, done.at[i]) for i, (a, b, c) in enumerate(routes)]
    outward = [pltpu.make_async_copy(b, c, done.at[2 + i]) for i, (a, b, c) in enumerate(routes)]
    for copy in inward:
        copy.start()
    for first, second in zip(inward, outward):
        first.wait()
        second.start()
    for copy in outward:
        copy.wait()


def local(
    rhs, inv_diag, face_coef, flux_jac, press_weights, surface_cells, interface_slot, mode_shapes
):
    n = lax.axis_size("space")
    planes, width = rhs.shape[2:]
    chunks = width // LANES
    rows, count = mode_shapes.shape
    tall = 2 * (rows // LANES)
    padded = -(-count // LANES) * LANES
    vmem = pl.BlockSpec(memory_space=pltpu.VMEM)
    hbm = pl.BlockSpec(memory_space=pltpu.HBM)
    smem = pl.BlockSpec(memory_space=pltpu.SMEM)
    f32 = jnp.float32
    dma = pltpu.SemaphoreType.DMA
    state, forces = pl.pallas_call(
        functools.partial(kernel, n),
        out_shape=(
            jax.ShapeDtypeStruct(rhs.shape, f32),
            jax.ShapeDtypeStruct((2, count // n), f32),
        ),
        in_specs=[smem, smem] + [hbm] * 6,
        out_specs=(vmem, vmem),
        scratch_shapes=[
            pltpu.VMEM(rhs.shape, f32),
            pltpu.VMEM(inv_diag.shape, f32),
            pltpu.VMEM(face_coef.shape, f32),
            pltpu.VMEM((1, rows), jnp.int32),
            pltpu.VMEM((1, rows), jnp.int32),
            pltpu.VMEM((count, rows), f32),
            dma((6,)),
            pltpu.VMEM((chunks + 2, 2 * COMP, planes, LANES), f32),
            pltpu.VMEM((chunks, 2 * COMP, planes, LANES), f32),
            pltpu.VMEM((4, chunks, planes, LANES), f32),
            pltpu.VMEM((ITERS // 2 + 1, 2, 2, 2 * COMP, chunks, LANES), f32),
            pltpu.VMEM((ITERS // 2, 2, 2, 2 * COMP, chunks, LANES), f32),
            pltpu.VMEM((2, 2 * COMP * (COMP + 1) + 4, chunks, LANES), f32),
            pltpu.VMEM((2, 2 * COMP * (COMP + 1) + 4, chunks, LANES), f32),
            pltpu.VMEM((2, 2 * COMP, chunks, LANES), f32),
            pltpu.VMEM((LANES, rows), jnp.bfloat16),
            pltpu.VMEM((chunks * planes, rows), f32),
            pltpu.VMEM((n * tall, rows), f32),
            pltpu.VMEM((LANES, rows), jnp.bfloat16),
            pltpu.VMEM((2, chunks, planes, LANES), f32),
            pltpu.VMEM((n, tall, LANES), f32),
            pltpu.VMEM((n, tall, LANES), f32),
            pltpu.VMEM((2, padded), f32),
            pltpu.VMEM((n, 2, padded), f32),
            dma((ITERS // 2, 2)), dma((ITERS // 2, 2)), dma((2,)), dma((2,)), dma((n,)), dma((n,)), dma((n,)), dma((n,)),
        ],
        compiler_params=pltpu.CompilerParams(
            collective_id=0, has_side_effects=True, vmem_limit_bytes=63 * 2**20
        ),
    )(
        flux_jac.transpose(1, 0, 2), press_weights, rhs, inv_diag, face_coef,
        surface_cells.reshape(1, rows), interface_slot.reshape(1, rows), mode_shapes.T,
    )
    return pl.pallas_call(
        hand_over,
        out_shape=(
            jax.ShapeDtypeStruct(state.shape, f32),
            jax.ShapeDtypeStruct(forces.shape, f32),
        ),
        in_specs=[hbm, hbm],
        out_specs=(hbm, hbm),
        scratch_shapes=[pltpu.VMEM(state.shape, f32), pltpu.VMEM(forces.shape, f32), dma((4,))],
        compiler_params=pltpu.CompilerParams(vmem_limit_bytes=63 * 2**20),
    )(state, forces)


def solution(mesh):
    in_specs = (
        P(None, None, ("freq", "space"), None),
        P(None, None, None, ("freq", "space"), None),
        P(None, ("freq", "space"), None),
        P(),
        P(),
        P("space"),
        P("space"),
        P("space", None),
    )
    out_specs = (P(None, None, ("freq", "space"), None), P(None, ("freq", "space")))
    return jax.shard_map(local, mesh=mesh, in_specs=in_specs, out_specs=out_specs, check_vma=False)
```

```python
import functools

import jax
import jax.numpy as jnp
from jax import lax
from jax.experimental import pallas as pl
from jax.experimental.pallas import tpu as pltpu
from jax.sharding import PartitionSpec as P

ITERS = 8
UNROLL = 4
LANES = 128
COMP = 5
MESH = pl.DeviceIdType.MESH


def log2(value):
    assert value & (value - 1) == 0
    return value.bit_length() - 1


def thirds(x):
    a = x.astype(jnp.bfloat16)
    rest = x - a.astype(jnp.float32)
    b = rest.astype(jnp.bfloat16)
    c = (rest - b.astype(jnp.float32)).astype(jnp.bfloat16)
    return jnp.concatenate([a, b, c], axis=0)


def dot_exact(x, onehot, dims):
    rows = x.shape[0]
    out = lax.dot_general(thirds(x), onehot, (dims, ((), ())), preferred_element_type=jnp.float32)
    return (out[:rows] + out[rows : 2 * rows]) + out[2 * rows :]


def kernel(
    n, flux, press, rhs_in, inv_in, face_in, cells_in, slots_in, modes_in, state_out, forces_out,
    rhs, inv, face, cells, slots, modes, loaded,
    held, mixed, masked, send, halo, fixed, beside, outer, pick, here, wanted, put,
    pressure, tiles, landed, part, parts,
    halo_send, halo_recv, fixed_send, fixed_recv,
    tile_send, tile_recv, part_send, part_recv,
):
    loads = [
        pltpu.make_async_copy(src, dst, loaded.at[i])
        for i, (src, dst) in enumerate(
            (
                (rhs_in, rhs), (inv_in, inv), (face_in, face),
                (cells_in, cells), (slots_in, slots), (modes_in, modes),
            )
        )
    ]
    for load in loads:
        load.start()
    planes, width = rhs.shape[2], rhs.shape[3]
    chunks = width // LANES
    rows = cells.shape[1]
    me = lax.axis_index("space")
    has_low, has_high = me > 0, me < n - 1

    barrier = pltpu.get_barrier_semaphore()

    def greet(d, carry):
        pl.semaphore_signal(
            barrier, inc=1, device_id={"space": lax.rem(me + d, n)}, device_id_type=MESH
        )
        return carry

    lax.fori_loop(1, n, greet, 0, unroll=True)

    row = lax.broadcasted_iota(jnp.int32, (planes, LANES), 0)
    lane = lax.broadcasted_iota(jnp.int32, (planes, LANES), 1)

    def at(c):
        return pl.ds(pl.multiple_of(c * LANES, LANES), LANES)

    def block_apply(block, z):
        reals, imags = [], []
        for k in range(COMP):
            real = imag = None
            for j in range(COMP):
                br, bi = block(k * COMP + j), block((COMP + k) * COMP + j)
                re = br * z[j] - bi * z[COMP + j]
                im = br * z[COMP + j] + bi * z[j]
                real = re if real is None else real + re
                imag = im if imag is None else imag + im
            reals.append(real)
            imags.append(imag)
        return reals + imags

    def own_block(c):
        return lambda i: inv[i // (COMP * COMP), i // COMP % COMP, i % COMP, :, at(c)]

    def keep(c, exchange, values):
        for f in range(2 * COMP):
            held[c + 1, f] = values[f]
            if exchange is not None:
                for p in range(2):
                    send[exchange, 0, p, f, pl.ds(c, 1)] = values[f][planes - 1 - p : planes - p]
                    send[exchange, 1, p, f, pl.ds(c, 1)] = values[f][p : p + 1]

    fields = 2 * COMP * COMP

    def first(c, carry):
        f0, f1 = face[0, :, at(c)], face[1, :, at(c)]
        zero = jnp.zeros_like(f0)
        masked[0, c] = jnp.where(row == planes - 1, zero, f0)
        masked[1, c] = jnp.where(row == 0, zero, f1)
        masked[2, c] = jnp.where(row == planes - 1, f0, zero)
        masked[3, c] = jnp.where(row == 0, f1, zero)
        z = [rhs[r, j, :, at(c)] for r in range(2) for j in range(COMP)]
        keep(c, 0, block_apply(own_block(c), z))
        block = own_block(c)
        f2, f3 = face[2, :, at(c)], face[3, :, at(c)]
        for i, x in enumerate([block(i) for i in range(fields)] + z):
            fixed[0, i, pl.ds(c, 1)] = x[planes - 1 :]
            fixed[1, i, pl.ds(c, 1)] = x[:1]
        for i, (x, y) in enumerate(((f0, f1), (f1, f0), (f2, f2), (f3, f3))):
            fixed[0, fields + 2 * COMP + i, pl.ds(c, 1)] = x[planes - 1 :]
            fixed[1, fields + 2 * COMP + i, pl.ds(c, 1)] = y[:1]
        return carry

    held[0] = jnp.zeros(held.shape[1:], jnp.float32)
    held[chunks + 1] = jnp.zeros(held.shape[1:], jnp.float32)

    @pl.when(jnp.logical_not(has_low))
    def _():
        beside[0] = jnp.zeros(beside.shape[1:], jnp.float32)
        for i in range(ITERS // 2):
            halo[i, 0] = jnp.zeros(halo.shape[2:], jnp.float32)

    @pl.when(jnp.logical_not(has_high))
    def _():
        beside[1] = jnp.zeros(beside.shape[1:], jnp.float32)
        for i in range(ITERS // 2):
            halo[i, 1] = jnp.zeros(halo.shape[2:], jnp.float32)

    for load in loads[:3]:
        load.wait()
    lax.fori_loop(0, chunks, first, 0, unroll=UNROLL)
    pl.semaphore_wait(barrier, n - 1)

    def state_copy(k, side, p):
        return pltpu.make_async_remote_copy(
            src_ref=send.at[k, side, p], dst_ref=halo.at[k, side, p],
            send_sem=halo_send.at[k, side, p], recv_sem=halo_recv.at[k, side, p],
            device_id={"space": me + 1 - 2 * side}, device_id_type=MESH,
        )

    def fixed_copy(side):
        return pltpu.make_async_remote_copy(
            src_ref=fixed.at[side], dst_ref=beside.at[side],
            send_sem=fixed_send.at[side], recv_sem=fixed_recv.at[side],
            device_id={"space": me + 1 - 2 * side}, device_id_type=MESH,
        )

    def exchange(k):
        for p in range(2):
            for side, there in ((0, has_high), (1, has_low)):
                pl.when(there)(state_copy(k, side, p).start)

    exchange(0)
    for side, there in ((0, has_high), (1, has_low)):
        pl.when(there)(fixed_copy(side).start)

    def before(c, carry):
        f0, f1 = masked[0, c], masked[1, c]
        f2, f3 = face[2, :, at(c)], face[3, :, at(c)]
        for r in range(2):
            planewise, cellwise = [], []
            for j in range(COMP):
                f = r * COMP + j
                own = held[c + 1, f]
                after = pltpu.roll(jnp.where(lane == 0, held[c + 2, f], own), LANES - 1, 1)
                ahead = pltpu.roll(jnp.where(lane == LANES - 1, held[c, f], own), 1, 1)
                cellwise.append(f2 * after + f3 * ahead)
                planewise.append(f0 * pltpu.roll(own, planes - 1, 0) + f1 * pltpu.roll(own, 1, 0))
            for k in range(COMP):
                total = rhs[r, k, :, at(c)]
                for j in range(COMP):
                    total += flux[k, 0, j] * planewise[j] + flux[k, 1, j] * cellwise[j]
                mixed[c, r * COMP + k] = total
        return carry

    def behind(c, low, high, exchange):
        e0, e1 = masked[2, c], masked[3, c]
        z = []
        for r in range(2):
            edge = [e1 * low(r * COMP + j, c) + e0 * high(r * COMP + j, c) for j in range(COMP)]
            for k in range(COMP):
                total = mixed[c, r * COMP + k]
                for j in range(COMP):
                    total += flux[k, 0, j] * edge[j]
                z.append(total)
        keep(c, exchange, block_apply(own_block(c), z))

    chunk_row = lax.broadcasted_iota(jnp.int32, (chunks, LANES), 0)
    chunk_lane = lax.broadcasted_iota(jnp.int32, (chunks, LANES), 1)
    first_cell = (chunk_row == 0) & (chunk_lane == 0)
    last_cell = (chunk_row == chunks - 1) & (chunk_lane == LANES - 1)

    def sweep_outer(s, side):
        coefs = [beside[side, fields + 2 * COMP + i] for i in range(4)]
        z = []
        for r in range(2):
            planewise, cellwise = [], []
            for j in range(COMP):
                f = r * COMP + j
                x = halo[s, side, 0, f]
                after = pltpu.roll(
                    jnp.where(chunk_lane == 0, pltpu.roll(x, chunks - 1, 0), x), LANES - 1, 1
                )
                ahead = pltpu.roll(
                    jnp.where(chunk_lane == LANES - 1, pltpu.roll(x, 1, 0), x), 1, 1
                )
                cellwise.append(
                    coefs[2] * jnp.where(last_cell, 0.0, after)
                    + coefs[3] * jnp.where(first_cell, 0.0, ahead)
                )
                planewise.append(
                    coefs[0] * send[s, 1 - side, 0, f] + coefs[1] * halo[s, side, 1, f]
                )
            for k in range(COMP):
                total = beside[side, fields + r * COMP + k]
                for j in range(COMP):
                    total += flux[k, 0, j] * planewise[j] + flux[k, 1, j] * cellwise[j]
                z.append(total)
        values = block_apply(lambda i: beside[side, i], z)
        for f in range(2 * COMP):
            outer[side, f] = values[f]

    def two_sweeps(s, carry):
        lax.fori_loop(0, chunks, before, 0, unroll=UNROLL)
        for there, come, gone in ((has_low, 0, 1), (has_high, 1, 0)):
            @pl.when(there)
            def _():
                state_copy(s, come, 0).wait_recv()

        def with_halo(c, inner):
            behind(
                c,
                lambda f, c: halo[s, 0, 0, f, pl.ds(c, 1)],
                lambda f, c: halo[s, 1, 0, f, pl.ds(c, 1)],
                None,
            )
            return inner

        lax.fori_loop(0, chunks, with_halo, 0, unroll=UNROLL)
        lax.fori_loop(0, chunks, before, 0, unroll=UNROLL)
        for there, come, gone in ((has_low, 0, 1), (has_high, 1, 0)):
            @pl.when(there)
            def _():
                state_copy(s, come, 1).wait_recv()
                state_copy(s, gone, 0).wait_send()
                state_copy(s, gone, 1).wait_send()

            @pl.when(there & (s == 0))
            def _():
                fixed_copy(come).wait_recv()
                fixed_copy(gone).wait_send()

        for side in range(2):
            sweep_outer(s, side)

        def with_outer(c, inner):
            behind(
                c,
                lambda f, c: outer[0, f, pl.ds(c, 1)],
                lambda f, c: outer[1, f, pl.ds(c, 1)],
                s + 1,
            )
            return inner

        lax.fori_loop(0, chunks, with_outer, 0, unroll=UNROLL)
        pl.when(s + 1 < ITERS // 2)(lambda: exchange(s + 1))
        return carry

    for load in loads[3:]:
        load.wait()
    cell, slot = cells[...], slots[...]
    grid = chunks * planes
    place = ((cell & (width - 1)) >> log2(LANES)) * planes + (cell >> log2(width))
    deep = rows // LANES
    tall = 2 * deep

    def count_rows(size):
        return lax.broadcasted_iota(jnp.int32, (size, rows), 0)

    def ones(where):
        return jnp.where(where, 1.0, 0.0)

    pick[...] = ones(count_rows(LANES) == (cell & (LANES - 1))).astype(jnp.bfloat16)
    put[...] = ones(count_rows(LANES) == (slot & (LANES - 1))).astype(jnp.bfloat16)
    here[...] = ones(count_rows(grid) == place)
    index = count_rows(n * tall)
    wanted[...] = ones(
        (index >> log2(tall)) * deep + (index & (deep - 1)) == (slot >> log2(LANES))
    )

    lax.fori_loop(0, ITERS // 2, two_sweeps, 0)

    def finish(c, carry):
        for r in range(2):
            total = None
            for j in range(COMP):
                value = held[c + 1, r * COMP + j]
                state_out[r, j, :, at(c)] = value
                term = press[j] * value
                total = term if total is None else total + term
            pressure[r, c] = total
        return carry

    lax.fori_loop(0, chunks, finish, 0, unroll=UNROLL)

    spread = dot_exact(pressure[...].reshape(2 * grid, LANES), pick[...], ((1,), (0,)))
    surface = [
        jnp.sum(here[...] * spread[r * grid : (r + 1) * grid], axis=0, keepdims=True)
        for r in range(2)
    ]
    value = wanted[...] * jnp.where(
        (count_rows(n * tall) & (tall - 1)) < deep, surface[0], surface[1]
    )
    tiles[...] = dot_exact(value, put[...], ((1,), (1,))).reshape(n, tall, LANES)

    def tile_copy(d):
        target = lax.rem(me + d, n)
        return pltpu.make_async_remote_copy(
            src_ref=tiles.at[target], dst_ref=landed.at[d],
            send_sem=tile_send.at[d], recv_sem=tile_recv.at[d],
            device_id={"space": target}, device_id_type=MESH,
        )

    def part_copy(d):
        return pltpu.make_async_remote_copy(
            src_ref=part, dst_ref=parts.at[d],
            send_sem=part_send.at[d], recv_sem=part_recv.at[d],
            device_id={"space": lax.rem(me + d, n)}, device_id_type=MESH,
        )

    def run(copy):
        def start(d, carry):
            copy(d).start()
            return carry

        def wait(d, carry):
            copy(d).wait()
            return carry

        lax.fori_loop(1, n, start, 0, unroll=True)
        lax.fori_loop(1, n, wait, 0, unroll=True)

    landed[0] = tiles[me]
    run(tile_copy)
    placed = jnp.sum(landed[...], axis=0)
    share = [None, None]
    for j in range(deep):
        product = lax.dot_general(
            placed, modes[:, j * LANES : (j + 1) * LANES], (((1,), (1,)), ((), ())),
            precision=lax.Precision.HIGHEST, preferred_element_type=jnp.float32,
        )
        for r in range(2):
            term = product[r * deep + j : r * deep + j + 1]
            share[r] = term if share[r] is None else share[r] + term
    count = modes.shape[0]
    part[...] = jnp.zeros(part.shape, jnp.float32)
    for r in range(2):
        part[r : r + 1, :count] = share[r]
    parts[0] = part[...]
    run(part_copy)
    total = jnp.sum(parts[...], axis=0)[:, :count]
    mine = forces_out.shape[1]
    choose = (
        lax.broadcasted_iota(jnp.int32, (count, mine), 0)
        == lax.broadcasted_iota(jnp.int32, (count, mine), 1) + me * mine
    )
    forces_out[...] = dot_exact(
        total, jnp.where(choose, 1.0, 0.0).astype(jnp.bfloat16), ((1,), (0,))
    )


def hand_over(state, forces, state_out, forces_out, state_held, forces_held, done):
    routes = ((state, state_held, state_out), (forces, forces_held, forces_out))
    inward = [pltpu.make_async_copy(a, b, done.at[i]) for i, (a, b, c) in enumerate(routes)]
    outward = [pltpu.make_async_copy(b, c, done.at[2 + i]) for i, (a, b, c) in enumerate(routes)]
    for copy in inward:
        copy.start()
    for first, second in zip(inward, outward):
        first.wait()
        second.start()
    for copy in outward:
        copy.wait()


def local(
    rhs, inv_diag, face_coef, flux_jac, press_weights, surface_cells, interface_slot, mode_shapes
):
    n = lax.axis_size("space")
    planes, width = rhs.shape[2:]
    chunks = width // LANES
    rows, count = mode_shapes.shape
    tall = 2 * (rows // LANES)
    padded = -(-count // LANES) * LANES
    vmem = pl.BlockSpec(memory_space=pltpu.VMEM)
    hbm = pl.BlockSpec(memory_space=pltpu.HBM)
    smem = pl.BlockSpec(memory_space=pltpu.SMEM)
    f32 = jnp.float32
    dma = pltpu.SemaphoreType.DMA
    state, forces = pl.pallas_call(
        functools.partial(kernel, n),
        out_shape=(
            jax.ShapeDtypeStruct(rhs.shape, f32),
            jax.ShapeDtypeStruct((2, count // n), f32),
        ),
        in_specs=[smem, smem] + [hbm] * 6,
        out_specs=(vmem, vmem),
        scratch_shapes=[
            pltpu.VMEM(rhs.shape, f32),
            pltpu.VMEM(inv_diag.shape, f32),
            pltpu.VMEM(face_coef.shape, f32),
            pltpu.VMEM((1, rows), jnp.int32),
            pltpu.VMEM((1, rows), jnp.int32),
            pltpu.VMEM((count, rows), f32),
            dma((6,)),
            pltpu.VMEM((chunks + 2, 2 * COMP, planes, LANES), f32),
            pltpu.VMEM((chunks, 2 * COMP, planes, LANES), f32),
            pltpu.VMEM((4, chunks, planes, LANES), f32),
            pltpu.VMEM((ITERS // 2 + 1, 2, 2, 2 * COMP, chunks, LANES), f32),
            pltpu.VMEM((ITERS // 2, 2, 2, 2 * COMP, chunks, LANES), f32),
            pltpu.VMEM((2, 2 * COMP * (COMP + 1) + 4, chunks, LANES), f32),
            pltpu.VMEM((2, 2 * COMP * (COMP + 1) + 4, chunks, LANES), f32),
            pltpu.VMEM((2, 2 * COMP, chunks, LANES), f32),
            pltpu.VMEM((LANES, rows), jnp.bfloat16),
            pltpu.VMEM((chunks * planes, rows), f32),
            pltpu.VMEM((n * tall, rows), f32),
            pltpu.VMEM((LANES, rows), jnp.bfloat16),
            pltpu.VMEM((2, chunks, planes, LANES), f32),
            pltpu.VMEM((n, tall, LANES), f32),
            pltpu.VMEM((n, tall, LANES), f32),
            pltpu.VMEM((2, padded), f32),
            pltpu.VMEM((n, 2, padded), f32),
            dma((ITERS // 2, 2, 2)), dma((ITERS // 2, 2, 2)), dma((2,)), dma((2,)), dma((n,)), dma((n,)), dma((n,)), dma((n,)),
        ],
        compiler_params=pltpu.CompilerParams(
            collective_id=0, has_side_effects=True, vmem_limit_bytes=63 * 2**20
        ),
    )(
        flux_jac.transpose(1, 0, 2), press_weights, rhs, inv_diag, face_coef,
        surface_cells.reshape(1, rows), interface_slot.reshape(1, rows), mode_shapes.T,
    )
    return pl.pallas_call(
        hand_over,
        out_shape=(
            jax.ShapeDtypeStruct(state.shape, f32),
            jax.ShapeDtypeStruct(forces.shape, f32),
        ),
        in_specs=[hbm, hbm],
        out_specs=(hbm, hbm),
        scratch_shapes=[pltpu.VMEM(state.shape, f32), pltpu.VMEM(forces.shape, f32), dma((4,))],
        compiler_params=pltpu.CompilerParams(vmem_limit_bytes=63 * 2**20),
    )(state, forces)


def solution(mesh):
    in_specs = (
        P(None, None, ("freq", "space"), None),
        P(None, None, None, ("freq", "space"), None),
        P(None, ("freq", "space"), None),
        P(),
        P(),
        P("space"),
        P("space"),
        P("space", None),
    )
    out_specs = (P(None, None, ("freq", "space"), None), P(None, ("freq", "space")))
    return jax.shard_map(local, mesh=mesh, in_specs=in_specs, out_specs=out_specs, check_vma=False)
```
